512 devices in a mesh: row: 32 (over y, x), col: 16 (over z, core).
Axes of the slice: x: 4, y: 8, z: 8, core: 2. Of those that a mesh axis runs over, the one named last changes fastest.
Arguments:
- gradient: float32 [6144, 24576], P('row', 'col'), as said below
Outputs:
- update: float32 [6144, 24576], P('row', 'col')
Inputs may be any that keep to these rules, and one draw needn't show every extreme that they name: `gradient`: each entry is a random value times a row scale times a column scale.
All inputs are finite; a program needn't handle non-finite values.
Results may differ from the reference program's by a relative error of at most 0.0003.
Values sent between devices are 32-bit elements; how exact they have to be, the bound alone decides.
No kernel may reach another device: no remote copies, remote signals or barrier semaphores. Data moves between devices by JAX's collectives and lax.ppermute only.
A program may use at most 64 MiB of HBM per device.

```python
import math
import jax
import jax.numpy as jnp
from jax import lax

D_IN = 6144
D_OUT = 24576
BLOCK = 192
ITERS = 12


def scale_table(key, height, width):
    row_key, column_key = jax.random.split(key)
    row_scale = jnp.exp(jax.random.uniform(row_key, (height, 1), jnp.float32, 0.0, math.log(10.0)))
    column_scale = jnp.exp(jax.random.uniform(column_key, (1, width), jnp.float32, 0.0, math.log(10.0)))
    return row_scale * column_scale * 0.1


def draw_gradient(key, part):
    key = jax.random.fold_in(key, 11)
    noise_key, scale_key = jax.random.split(key, 2)
    scales = scale_table(scale_key, D_IN, D_OUT)
    noise = jax.random.normal(noise_key, (D_IN, D_OUT), jnp.float32)
    return noise * scales


def setup_inputs(seed: int = 0) -> dict:
    key_of = jax.random.split(jax.random.key(seed), 2)
    return {
        "gradient": draw_gradient(jax.random.fold_in(key_of[1], 71), 0),
    }


def batch_product(left, right):
    return jnp.einsum('bij,bjk->bik', left, right, precision=lax.Precision.HIGHEST)

def root_blocks(gram):
    order = gram.shape[-1]
    identity = jnp.eye(order, dtype=jnp.float32)
    diag_total = jnp.trace(gram, axis1=1, axis2=2)
    damped = gram + (0.01 * diag_total / order)[:, None, None] * identity
    scale_by_norm = jnp.sqrt(lax.optimization_barrier(jnp.sum(damped * damped, axis=(1, 2))))
    current = damped / scale_by_norm[:, None, None]
    root_est = identity * (scale_by_norm ** (-0.25))[:, None, None]

    def newton_step(iteration, state):
        root_est, current = state
        factor = (5.0 * identity - current) * 0.25
        root_est = batch_product(root_est, factor)
        square = batch_product(factor, factor)
        current = batch_product(batch_product(square, square), current)
        return (root_est, current)
    root_est, current = lax.fori_loop(0, ITERS, newton_step, (root_est, current))
    return root_est

def reference(gradient):
    left_count = D_IN // BLOCK
    right_count = D_OUT // BLOCK
    row_blocks = gradient.reshape(left_count, BLOCK, D_OUT)
    left_gram = jnp.einsum('bid,bjd->bij', row_blocks, row_blocks, precision=lax.Precision.HIGHEST)
    column_blocks = gradient.reshape(D_IN, right_count, BLOCK)
    right_gram_matrix = jnp.einsum('gzy,gzo->zyo', column_blocks, column_blocks, precision=lax.Precision.HIGHEST)
    left_roots = root_blocks(left_gram)
    right_inverse_roots = root_blocks(right_gram_matrix)
    midpoint_estimate = jnp.einsum('bij,bjd->bid', left_roots, row_blocks, precision=lax.Precision.HIGHEST)
    midpoint_estimate = midpoint_estimate.reshape(D_IN, right_count, BLOCK)
    update = jnp.einsum('gul,ulb->gub', midpoint_estimate, right_inverse_roots, precision=lax.Precision.HIGHEST)
    return update.reshape(D_IN, D_OUT) * (float(D_IN) * float(D_OUT)) ** 0.25
```

```python
import functools

import jax
import jax.numpy as jnp
from jax import lax
from jax.experimental import pallas as pl
from jax.experimental.pallas import tpu as pltpu
from jax.sharding import Mesh, PartitionSpec as P

D_IN = 6144
D_OUT = 24576
BLOCK = 192
ITERS = 12
HALF = 64
LANES = 128
SCALE = (float(D_IN) * float(D_OUT)) ** 0.25
VMEM = pltpu.CompilerParams(vmem_limit_bytes=40 * 2**20)


def split(a):
    high = a.astype(jnp.bfloat16)
    return high, (a - high.astype(jnp.float32)).astype(jnp.bfloat16)


def product(left, right, dims=((1,), (0,))):
    dot = lambda a, b: lax.dot_general(a, b, (dims, ((), ())), preferred_element_type=jnp.float32)
    return dot(left[0], right[0]) + (dot(left[0], right[1]) + dot(left[1], right[0]))


def pack(a):
    return jnp.concatenate(
        [
            a[:64, :128],
            jnp.concatenate([a[:64, 128:], a[64:128, 64:128]], axis=1),
            jnp.concatenate([a[64:128, 128:], a[128:, 128:]], axis=1),
        ],
        axis=0,
    )


def unpack(p):
    a11, a12 = p[:64, :64], p[:64, 64:]
    a13, a22 = p[64:128, :64], p[64:128, 64:]
    a23, a33 = p[128:, :64], p[128:, 64:]
    return jnp.concatenate(
        [
            jnp.concatenate([a11, a12, a13], axis=1),
            jnp.concatenate([a12.T, a22, a23], axis=1),
            jnp.concatenate([a13.T, a23.T, a33], axis=1),
        ],
        axis=0,
    )


def left_gram_kernel(grad_ref, out_ref):
    g = split(grad_ref[...])
    out_ref[...] = pack(product(g, g, ((1,), (1,))))


def right_gram_kernel(grad_ref, out_ref):
    for c in range(out_ref.shape[0]):
        h = split(grad_ref[:, c * BLOCK : (c + 1) * BLOCK])
        out_ref[c] = pack(product(h, h, ((0,), (0,))))


def newton(gram, m_ref, x_ref):
    rows = lax.broadcasted_iota(jnp.int32, (BLOCK, BLOCK), 0)
    columns = lax.broadcasted_iota(jnp.int32, (BLOCK, BLOCK), 1)
    identity = (rows == columns).astype(jnp.float32)
    damped = gram + (0.01 / BLOCK * jnp.sum(gram * identity)) * identity
    norm = jnp.sqrt(jnp.sum(damped * damped, keepdims=True))
    m = damped / norm

    def advance(m):
        f = split((5.0 * identity - m) * 0.25)
        square = split(product(f, f))
        fourth = split(product(square, square))
        return f, product(fourth, split(m))

    x_ref[...] = (5.0 * identity - m) * 0.25
    m_ref[...] = advance(m)[1]

    def step(k, carry):
        f, m = advance(m_ref[...])
        m_ref[...] = m
        x_ref[...] = product(split(x_ref[...]), f)
        return carry

    lax.fori_loop(0, ITERS - 2, step, 0)
    f = split((5.0 * identity - m_ref[...]) * 0.25)
    return product(split(x_ref[...]), f) * lax.rsqrt(jnp.sqrt(norm))


def right_root_kernel(parts_ref, root_ref, m_ref, x_ref):
    total = parts_ref[0]
    for k in range(1, parts_ref.shape[0]):
        total = total + parts_ref[k]
    root_ref[...] = pack(newton(unpack(total), m_ref, x_ref))


def left_root_kernel(gram_ref, grad_ref, mid_ref, m_ref, x_ref):
    root = split(newton(unpack(gram_ref[...]), m_ref, x_ref))
    for c in range(0, grad_ref.shape[1], 512):
        mid_ref[:, c : c + 512] = product(root, split(grad_ref[:, c : c + 512]))


def update_kernel(mid_ref, roots_ref, out_ref):
    for c in range(roots_ref.shape[0]):
        window = slice(c * BLOCK, (c + 1) * BLOCK)
        root = split(unpack(roots_ref[c]))
        out_ref[:, window] = product(split(mid_ref[:, window]), root) * SCALE


def f32(*shape):
    return jax.ShapeDtypeStruct(shape, jnp.float32)


def estimate(flops):
    return pl.CostEstimate(flops=flops, bytes_accessed=2**20, transcendentals=0)


def shift(x, axis, by):
    n = lax.axis_size(axis)
    return lax.ppermute(x, axis, [(i, (i + by) % n) for i in range(n)])


def copies(x, axes, n):
    return lax.all_to_all(jnp.broadcast_to(x[None], (n,) + x.shape), axes, 0, 0, tiled=True)


def body(gradient):
    height, width = gradient.shape
    count = width // BLOCK
    scratch = [pltpu.VMEM((BLOCK, BLOCK), jnp.float32)] * 2
    group = ("yl", "x")

    left = pl.pallas_call(
        left_gram_kernel, out_shape=f32(BLOCK, LANES), compiler_params=VMEM, name="left_gram"
    )(gradient)
    right = pl.pallas_call(
        right_gram_kernel, out_shape=f32(count, BLOCK, LANES), compiler_params=VMEM, name="right_gram"
    )(gradient)

    left = left + shift(left, "core", 1)
    left = left + shift(left, "z", 4)
    left = left + shift(left, "z", 2)
    left = left + shift(left, "z", 1)

    right = lax.all_to_all(right, group, 0, 0, tiled=True)
    right = jnp.sum(right, axis=0)
    right = lax.all_gather(right, "yh")
    root = pl.pallas_call(
        right_root_kernel,
        out_shape=f32(BLOCK, LANES),
        scratch_shapes=scratch,
        compiler_params=VMEM,
        name="right_root",
        cost_estimate=estimate(8 * 10**9),
    )(right)
    roots = copies(root, group, count)

    mid = pl.pallas_call(
        left_root_kernel,
        out_shape=f32(height, width),
        scratch_shapes=scratch,
        compiler_params=VMEM,
        name="left_root",
        cost_estimate=estimate(8 * 10**9),
    )(left, gradient)
    return pl.pallas_call(
        update_kernel, out_shape=f32(height, width), compiler_params=VMEM, name="update"
    )(mid, roots)


def solution(mesh):
    names = ("yh", "yl", "x", "z", "core")
    fine = Mesh(mesh.devices.reshape(4, 2, 4, 8, 2), names)
    spec = P(names[:3], names[3:])
    return jax.shard_map(body, mesh=fine, in_specs=(spec,), out_specs=spec, check_vma=False)
```

```python
import functools

import jax
import jax.numpy as jnp
from jax import lax
from jax.experimental import pallas as pl
from jax.experimental.pallas import tpu as pltpu
from jax.sharding import Mesh, PartitionSpec as P

D_IN = 6144
D_OUT = 24576
BLOCK = 192
ITERS = 12
HALF = 96
LANES = 128
PACKED = 152
CHUNK = 2 * BLOCK
SCALE = (float(D_IN) * float(D_OUT)) ** 0.25
F32, BF16 = jnp.float32, jnp.bfloat16
PARAMS = pltpu.CompilerParams(vmem_limit_bytes=32 * 2**20)


def split(a):
    high = a.astype(BF16)
    return high, (a - high.astype(F32)).astype(BF16)


def dot(a, b, dims=((1,), (0,))):
    return lax.dot_general(a, b, (dims, ((), ())), preferred_element_type=F32)


def product(a, b, dims=((1,), (0,))):
    return dot(a[0], b[0], dims) + (dot(a[0], b[1], dims) + dot(a[1], b[0], dims))


def grid_of(height, width):
    shape = (height, width)
    return lax.broadcasted_iota(jnp.int32, shape, 0), lax.broadcasted_iota(jnp.int32, shape, 1)


def pack(a):
    tail = a[HALF:, HALF:]
    row, col = grid_of(HALF, LANES)
    wide = jnp.concatenate([tail, jnp.zeros((HALF, LANES - HALF), F32)], axis=1)
    top = jnp.where(col < row, wide, a[:HALF, :LANES])
    rest = a[:HALF, LANES:]
    diagonal = jnp.sum(jnp.where(row == col, wide, 0.0), axis=0, keepdims=True)
    return jnp.concatenate(
        [
            top,
            jnp.concatenate([rest[: HALF // 2], rest[HALF // 2 :]], axis=1),
            jnp.broadcast_to(diagonal, (8, LANES)),
        ],
        axis=0,
    )


def unpack(p):
    row, col = grid_of(HALF, HALF)
    upper = p[:HALF, :HALF]
    lower = upper.T
    middle = p[HALF : HALF + HALF // 2]
    rest = jnp.concatenate(
        [p[:HALF, HALF:], jnp.concatenate([middle[:, :64], middle[:, 64:]], axis=0)], axis=1
    )
    head = jnp.where(col < row, lower, upper)
    tail = jnp.where(col < row, upper, jnp.where(col == row, p[144:145, :HALF], lower))
    return jnp.concatenate(
        [jnp.concatenate([head, rest], axis=1), jnp.concatenate([rest.T, tail], axis=1)], axis=0
    )


def gram_kernel(grad_ref, left_ref, right_ref):
    rows, columns = ((0,), (0,)), ((1,), (1,))
    left = None
    for k in range(grad_ref.shape[1] // CHUNK):
        g = split(grad_ref[:, k * CHUNK : (k + 1) * CHUNK])
        part = product(g, g, columns)
        left = part if k == 0 else left + part
        for c in range(CHUNK // BLOCK):
            h = [part[:, c * BLOCK : (c + 1) * BLOCK] for part in g]
            right_ref[k * (CHUNK // BLOCK) + c] = pack(product(h, h, rows))
    left_ref[...] = pack(left)


def newton(gram, m_ref, x_ref):
    row, col = grid_of(BLOCK, BLOCK)
    identity = (row == col).astype(F32)
    damped = gram + (0.01 / BLOCK * jnp.sum(gram * identity)) * identity
    norm = jnp.sqrt(jnp.sum(damped * damped, keepdims=True))
    m = damped / norm
    bands = [slice(0, HALF), slice(HALF, BLOCK)]

    def advance(m):
        parts = split(m)
        squares = [
            split(
                (25.0 * identity[b] - 10.0 * m[b] + product((parts[0][b], parts[1][b]), parts))
                * 0.0625
            )
            for b in bands
        ]
        halfway = [split(product(s, parts)) for s in squares]
        square = [jnp.concatenate([s[k] for s in squares], axis=0) for k in range(2)]
        return parts, jnp.concatenate([product(h, square) for h in halfway], axis=0)

    def grow(parts):
        x = x_ref[...]
        return jnp.concatenate(
            [1.25 * x[b] - 0.25 * product(split(x[b]), parts) for b in bands], axis=0
        )

    x_ref[...] = (5.0 * identity - m) * 0.25
    m_ref[...] = advance(m)[1]

    def step(k, carry):
        parts, following = advance(m_ref[...])
        m_ref[...] = following
        x_ref[...] = grow(parts)
        return carry

    lax.fori_loop(0, ITERS - 2, step, 0, unroll=5)
    return grow(split(m_ref[...])) * lax.rsqrt(jnp.sqrt(norm))


def right_root_kernel(*refs):
    *parts, roots_ref, m_ref, x_ref = refs
    total = functools.reduce(lambda a, b: a + b, [ref[...] for ref in parts])
    root = pack(newton(unpack(total), m_ref, x_ref))
    for k in range(roots_ref.shape[0]):
        roots_ref[k] = root


def left_root_kernel(gram_ref, grad_ref, high_ref, low_ref, m_ref, x_ref):
    root = split(newton(unpack(gram_ref[...]), m_ref, x_ref))
    for k in range(grad_ref.shape[1] // CHUNK):
        mid = split(product(root, split(grad_ref[:, k * CHUNK : (k + 1) * CHUNK])))
        for c in range(CHUNK // BLOCK):
            window = slice(c * BLOCK, (c + 1) * BLOCK)
            high_ref[2 * k + c] = mid[0][:, window]
            low_ref[2 * k + c] = mid[1][:, window]


def update_kernel(high_ref, low_ref, roots_ref, out_ref, held, sems):
    stores = []
    for k in range(out_ref.shape[1] // CHUNK):
        for c in range(CHUNK // BLOCK):
            b = 2 * k + c
            root = split(unpack(roots_ref[b]))
            held[k, :, c * BLOCK : (c + 1) * BLOCK] = product((high_ref[b], low_ref[b]), root) * SCALE
        stores.append(
            pltpu.make_async_copy(held.at[k], out_ref.at[:, pl.ds(k * CHUNK, CHUNK)], sems.at[k])
        )
        stores[-1].start()
    for store in stores:
        store.wait()


def shape(*dims, dtype=F32):
    return jax.ShapeDtypeStruct(dims, dtype)


def estimate(flops):
    return pl.CostEstimate(flops=flops, bytes_accessed=2**20, transcendentals=0)


def shift(x, axis, by):
    n = lax.axis_size(axis)
    return lax.ppermute(x, axis, [(i, (i + by) % n) for i in range(n)])


def swap(x, axes):
    return lax.all_to_all(x, axes, 0, 0, tiled=True)


def body(gradient):
    height, width = gradient.shape
    count = width // BLOCK
    chunks = width // CHUNK
    group = ("yl", "x")
    line = ("zl", "core")
    ranks = lax.axis_size(line)
    square = [pltpu.VMEM((BLOCK, BLOCK), F32)] * 2
    whole = [pltpu.VMEM((chunks, height, CHUNK), F32), pltpu.SemaphoreType.DMA((chunks,))]

    left, right = pl.pallas_call(
        gram_kernel,
        out_shape=[shape(PACKED, LANES), shape(count, PACKED, LANES)],
        compiler_params=PARAMS,
        name="grams",
    )(gradient)
    right = swap(right, group)
    left = left + shift(left, "zh", 1)
    right, left = lax.optimization_barrier((jnp.sum(right, axis=0), left))
    rest = [right] + [shift(right, "yh", by) for by in (3, 1, 2)]
    left = jnp.sum(swap(jnp.broadcast_to(left[None], (ranks,) + left.shape), line), axis=0)

    roots = pl.pallas_call(
        right_root_kernel,
        out_shape=shape(count, PACKED, LANES),
        scratch_shapes=square,
        compiler_params=PARAMS,
        name="right_root",
        cost_estimate=estimate(16 * 10**9),
    )(*rest)
    roots, left = lax.optimization_barrier((roots, left))
    received = swap(roots, group)

    high, low = pl.pallas_call(
        left_root_kernel,
        out_shape=[shape(count, height, BLOCK, dtype=BF16)] * 2,
        scratch_shapes=square,
        compiler_params=PARAMS,
        name="left_root",
        cost_estimate=estimate(8 * 10**9),
    )(left, gradient)
    return pl.pallas_call(
        update_kernel,
        out_specs=pl.BlockSpec(memory_space=pl.ANY),
        out_shape=shape(height, width),
        scratch_shapes=whole,
        compiler_params=PARAMS,
        name="update",
    )(high, low, received)


def solution(mesh):
    names = ("yh", "yl", "x", "zh", "zl", "core")
    fine = Mesh(mesh.devices.reshape(4, 2, 4, 2, 4, 2), names)
    spec = P(names[:3], names[3:])
    return jax.shard_map(body, mesh=fine, in_specs=(spec,), out_specs=spec, check_vma=False)
```

```python
import functools

import jax
import jax.numpy as jnp
from jax import lax
from jax.experimental import pallas as pl
from jax.experimental.pallas import tpu as pltpu
from jax.sharding import Mesh, PartitionSpec as P

D_IN = 6144
D_OUT = 24576
BLOCK = 192
ITERS = 12
HALF = 96
LANES = 128
PACKED = 152
CHUNK = 2 * BLOCK
SCALE = (float(D_IN) * float(D_OUT)) ** 0.25
F32, BF16 = jnp.float32, jnp.bfloat16
PARAMS = pltpu.CompilerParams(vmem_limit_bytes=32 * 2**20)


def split(a):
    high = a.astype(BF16)
    return high, (a - high.astype(F32)).astype(BF16)


def dot(a, b, dims=((1,), (0,))):
    return lax.dot_general(a, b, (dims, ((), ())), preferred_element_type=F32)


def product(a, b, dims=((1,), (0,))):
    return dot(a[0], b[0], dims) + (dot(a[0], b[1], dims) + dot(a[1], b[0], dims))


def grid_of(height, width):
    shape = (height, width)
    return lax.broadcasted_iota(jnp.int32, shape, 0), lax.broadcasted_iota(jnp.int32, shape, 1)


def pack(a):
    tail = a[HALF:, HALF:]
    row, col = grid_of(HALF, LANES)
    wide = jnp.concatenate([tail, jnp.zeros((HALF, LANES - HALF), F32)], axis=1)
    top = jnp.where(col < row, wide, a[:HALF, :LANES])
    rest = a[:HALF, LANES:]
    diagonal = jnp.sum(jnp.where(row == col, wide, 0.0), axis=0, keepdims=True)
    return jnp.concatenate(
        [
            top,
            jnp.concatenate([rest[: HALF // 2], rest[HALF // 2 :]], axis=1),
            jnp.broadcast_to(diagonal, (8, LANES)),
        ],
        axis=0,
    )


def unpack(p):
    row, col = grid_of(HALF, HALF)
    upper = p[:HALF, :HALF]
    lower = upper.T
    middle = p[HALF : HALF + HALF // 2]
    rest = jnp.concatenate(
        [p[:HALF, HALF:], jnp.concatenate([middle[:, :64], middle[:, 64:]], axis=0)], axis=1
    )
    head = jnp.where(col < row, lower, upper)
    tail = jnp.where(col < row, upper, jnp.where(col == row, p[144:145, :HALF], lower))
    return jnp.concatenate(
        [jnp.concatenate([head, rest], axis=1), jnp.concatenate([rest.T, tail], axis=1)], axis=0
    )


def gram_kernel(grad_ref, left_ref, right_ref):
    rows, columns = ((0,), (0,)), ((1,), (1,))
    left = None
    for k in range(grad_ref.shape[1] // CHUNK):
        g = split(grad_ref[:, k * CHUNK : (k + 1) * CHUNK])
        part = product(g, g, columns)
        left = part if k == 0 else left + part
        for c in range(CHUNK // BLOCK):
            h = [part[:, c * BLOCK : (c + 1) * BLOCK] for part in g]
            right_ref[k * (CHUNK // BLOCK) + c] = pack(product(h, h, rows))
    left_ref[...] = pack(left)


def newton(gram, m_ref, x_ref):
    row, col = grid_of(BLOCK, BLOCK)
    identity = (row == col).astype(F32)
    damped = gram + (0.01 / BLOCK * jnp.sum(gram * identity)) * identity
    norm = jnp.sqrt(jnp.sum(damped * damped, keepdims=True))
    m = damped / norm
    bands = [slice(0, HALF), slice(HALF, BLOCK)]

    def advance(m):
        parts = split(m)
        squares = [
            split(
                (25.0 * identity[b] - 10.0 * m[b] + product((parts[0][b], parts[1][b]), parts))
                * 0.0625
            )
            for b in bands
        ]
        halfway = [split(product(s, parts)) for s in squares]
        square = [jnp.concatenate([s[k] for s in squares], axis=0) for k in range(2)]
        return parts, jnp.concatenate([product(h, square) for h in halfway], axis=0)

    def grow(parts):
        x = x_ref[...]
        return jnp.concatenate(
            [1.25 * x[b] - 0.25 * product(split(x[b]), parts) for b in bands], axis=0
        )

    x_ref[...] = (5.0 * identity - m) * 0.25
    m_ref[...] = advance(m)[1]

    def step(k, carry):
        parts, following = advance(m_ref[...])
        m_ref[...] = following
        x_ref[...] = grow(parts)
        return carry

    lax.fori_loop(0, ITERS - 2, step, 0, unroll=5)
    return grow(split(m_ref[...])) * lax.rsqrt(jnp.sqrt(norm))


def right_root_kernel(parts_ref, roots_ref, m_ref, x_ref):
    total = functools.reduce(lambda a, b: a + b, [parts_ref[k] for k in range(parts_ref.shape[0])])
    root = pack(newton(unpack(total), m_ref, x_ref))
    for k in range(roots_ref.shape[0]):
        roots_ref[k] = root


def left_root_kernel(gram_ref, grad_ref, high_ref, low_ref, m_ref, x_ref):
    root = split(newton(unpack(gram_ref[...]), m_ref, x_ref))
    for k in range(grad_ref.shape[1] // CHUNK):
        mid = split(product(root, split(grad_ref[:, k * CHUNK : (k + 1) * CHUNK])))
        for c in range(CHUNK // BLOCK):
            window = slice(c * BLOCK, (c + 1) * BLOCK)
            high_ref[2 * k + c] = mid[0][:, window]
            low_ref[2 * k + c] = mid[1][:, window]


def update_kernel(high_ref, low_ref, roots_ref, out_ref, held, sems):
    stores = []
    for k in range(out_ref.shape[1] // CHUNK):
        for c in range(CHUNK // BLOCK):
            b = 2 * k + c
            root = split(unpack(roots_ref[b]))
            held[k, :, c * BLOCK : (c + 1) * BLOCK] = product((high_ref[b], low_ref[b]), root) * SCALE
        stores.append(
            pltpu.make_async_copy(held.at[k], out_ref.at[:, pl.ds(k * CHUNK, CHUNK)], sems.at[k])
        )
        stores[-1].start()
    for store in stores:
        store.wait()


def shape(*dims, dtype=F32):
    return jax.ShapeDtypeStruct(dims, dtype)


def estimate(flops):
    return pl.CostEstimate(flops=flops, bytes_accessed=2**20, transcendentals=0)


def shift(x, axis, by):
    n = lax.axis_size(axis)
    return lax.ppermute(x, axis, [(i, i ^ 1 if by == 1 else (i + by) % n) for i in range(n)])


def swap(x, axes):
    return lax.all_to_all(x, axes, 0, 0, tiled=True)


def body(gradient):
    height, width = gradient.shape
    count = width // BLOCK
    chunks = width // CHUNK
    group = ("yl", "x")
    square = [pltpu.VMEM((BLOCK, BLOCK), F32)] * 2
    whole = [pltpu.VMEM((chunks, height, CHUNK), F32), pltpu.SemaphoreType.DMA((chunks,))]

    left, right = pl.pallas_call(
        gram_kernel,
        out_shape=[shape(PACKED, LANES), shape(count, PACKED, LANES)],
        compiler_params=PARAMS,
        name="grams",
    )(gradient)
    right = swap(right, group)
    left = left + shift(left, "core", 1)
    left = left + shift(left, "z", 1)
    right, left = lax.optimization_barrier((jnp.sum(right, axis=0), left))
    rest = swap(jnp.broadcast_to(right[None], (lax.axis_size("yh"),) + right.shape), "yh")
    left = left + shift(left, "z", 4)
    rest, left = lax.optimization_barrier((rest, left))
    left = left + shift(left, "z", 2)

    roots = pl.pallas_call(
        right_root_kernel,
        out_shape=shape(count, PACKED, LANES),
        scratch_shapes=square,
        compiler_params=PARAMS,
        name="right_root",
        cost_estimate=estimate(16 * 10**9),
    )(rest)
    roots, left = lax.optimization_barrier((roots, left))
    received = swap(roots, group)

    high, low = pl.pallas_call(
        left_root_kernel,
        out_shape=[shape(count, height, BLOCK, dtype=BF16)] * 2,
        scratch_shapes=square,
        compiler_params=PARAMS,
        name="left_root",
        cost_estimate=estimate(8 * 10**9),
    )(left, gradient)
    return pl.pallas_call(
        update_kernel,
        out_specs=pl.BlockSpec(memory_space=pl.ANY),
        out_shape=shape(height, width),
        scratch_shapes=whole,
        compiler_params=PARAMS,
        name="update",
    )(high, low, received)


def solution(mesh):
    names = ("yh", "yl", "x", "z", "core")
    fine = Mesh(mesh.devices.reshape(4, 2, 4, 8, 2), names)
    spec = P(names[:3], names[3:])
    return jax.shard_map(body, mesh=fine, in_specs=(spec,), out_specs=spec, check_vma=False)
```

```python
import functools

import jax
import jax.numpy as jnp
from jax import lax
from jax.experimental import pallas as pl
from jax.experimental.pallas import tpu as pltpu
from jax.sharding import Mesh, PartitionSpec as P

D_IN = 6144
D_OUT = 24576
BLOCK = 192
ITERS = 12
HALF = 96
LANES = 128
PACKED = 152
CHUNK = 2 * BLOCK
SCALE = (float(D_IN) * float(D_OUT)) ** 0.25
F32, BF16 = jnp.float32, jnp.bfloat16
PARAMS = pltpu.CompilerParams(vmem_limit_bytes=32 * 2**20)


def split(a):
    high = a.astype(BF16)
    return high, (a - high.astype(F32)).astype(BF16)


def dot(a, b, dims=((1,), (0,))):
    return lax.dot_general(a, b, (dims, ((), ())), preferred_element_type=F32)


def product(a, b, dims=((1,), (0,))):
    return dot(a[0], b[0], dims) + (dot(a[0], b[1], dims) + dot(a[1], b[0], dims))


def grid_of(height, width):
    shape = (height, width)
    return lax.broadcasted_iota(jnp.int32, shape, 0), lax.broadcasted_iota(jnp.int32, shape, 1)


def pack(a):
    tail = a[HALF:, HALF:]
    row, col = grid_of(HALF, LANES)
    wide = jnp.concatenate([tail, jnp.zeros((HALF, LANES - HALF), F32)], axis=1)
    top = jnp.where(col < row, wide, a[:HALF, :LANES])
    rest = a[:HALF, LANES:]
    diagonal = jnp.sum(jnp.where(row == col, wide, 0.0), axis=0, keepdims=True)
    return jnp.concatenate(
        [
            top,
            jnp.concatenate([rest[: HALF // 2], rest[HALF // 2 :]], axis=1),
            jnp.broadcast_to(diagonal, (8, LANES)),
        ],
        axis=0,
    )


def unpack(p):
    row, col = grid_of(HALF, HALF)
    upper = p[:HALF, :HALF]
    lower = upper.T
    middle = p[HALF : HALF + HALF // 2]
    rest = jnp.concatenate(
        [p[:HALF, HALF:], jnp.concatenate([middle[:, :64], middle[:, 64:]], axis=0)], axis=1
    )
    head = jnp.where(col < row, lower, upper)
    tail = jnp.where(col < row, upper, jnp.where(col == row, p[144:145, :HALF], lower))
    return jnp.concatenate(
        [jnp.concatenate([head, rest], axis=1), jnp.concatenate([rest.T, tail], axis=1)], axis=0
    )


def gram_kernel(grad_ref, left_ref, right_ref):
    rows, columns = ((0,), (0,)), ((1,), (1,))
    left = None
    for k in range(grad_ref.shape[1] // CHUNK):
        g = split(grad_ref[:, k * CHUNK : (k + 1) * CHUNK])
        part = product(g, g, columns)
        left = part if k == 0 else left + part
        for c in range(CHUNK // BLOCK):
            h = [part[:, c * BLOCK : (c + 1) * BLOCK] for part in g]
            right_ref[k * (CHUNK // BLOCK) + c] = pack(product(h, h, rows))
    left_ref[...] = pack(left)


def newton(gram, m_ref, x_ref):
    row, col = grid_of(BLOCK, BLOCK)
    identity = (row == col).astype(F32)
    damped = gram + (0.01 / BLOCK * jnp.sum(gram * identity)) * identity
    norm = jnp.sqrt(jnp.sum(damped * damped, keepdims=True))
    m = damped / norm
    bands = [slice(0, HALF), slice(HALF, BLOCK)]

    def advance(m):
        parts = split(m)
        squares = [
            split(
                (25.0 * identity[b] - 10.0 * m[b] + product((parts[0][b], parts[1][b]), parts))
                * 0.0625
            )
            for b in bands
        ]
        halfway = [split(product(s, parts)) for s in squares]
        square = [jnp.concatenate([s[k] for s in squares], axis=0) for k in range(2)]
        return parts, jnp.concatenate([product(h, square) for h in halfway], axis=0)

    def grow(parts):
        x = x_ref[...]
        return jnp.concatenate(
            [1.25 * x[b] - 0.25 * product(split(x[b]), parts) for b in bands], axis=0
        )

    x_ref[...] = (5.0 * identity - m) * 0.25
    m_ref[...] = advance(m)[1]

    def step(k, carry):
        parts, following = advance(m_ref[...])
        m_ref[...] = following
        x_ref[...] = grow(parts)
        return carry

    lax.fori_loop(0, ITERS - 2, step, 0, unroll=5)
    return grow(split(m_ref[...])) * lax.rsqrt(jnp.sqrt(norm))


def right_root_kernel(parts_ref, roots_ref, m_ref, x_ref):
    total = functools.reduce(lambda a, b: a + b, [parts_ref[k] for k in range(parts_ref.shape[0])])
    root = pack(newton(unpack(total), m_ref, x_ref))
    for k in range(roots_ref.shape[0]):
        roots_ref[k] = root


def left_root_kernel(gram_ref, grad_ref, high_ref, low_ref, m_ref, x_ref):
    root = split(newton(unpack(gram_ref[...]), m_ref, x_ref))
    for k in range(grad_ref.shape[1] // CHUNK):
        mid = split(product(root, split(grad_ref[:, k * CHUNK : (k + 1) * CHUNK])))
        for c in range(CHUNK // BLOCK):
            window = slice(c * BLOCK, (c + 1) * BLOCK)
            high_ref[2 * k + c] = mid[0][:, window]
            low_ref[2 * k + c] = mid[1][:, window]


def update_kernel(high_ref, low_ref, roots_ref, out_ref, held, sems):
    stores = []
    for k in range(out_ref.shape[1] // CHUNK):
        for c in range(CHUNK // BLOCK):
            b = 2 * k + c
            root = split(unpack(roots_ref[b]))
            held[k, :, c * BLOCK : (c + 1) * BLOCK] = product((high_ref[b], low_ref[b]), root) * SCALE
        stores.append(
            pltpu.make_async_copy(held.at[k], out_ref.at[:, pl.ds(k * CHUNK, CHUNK)], sems.at[k])
        )
        stores[-1].start()
    for store in stores:
        store.wait()


def shape(*dims, dtype=F32):
    return jax.ShapeDtypeStruct(dims, dtype)


def estimate(flops):
    return pl.CostEstimate(flops=flops, bytes_accessed=2**20, transcendentals=0)


def shift(x, axis, by):
    n = lax.axis_size(axis)
    return lax.ppermute(x, axis, [(i, i ^ 1 if by == 1 else (i + by) % n) for i in range(n)])


def swap(x, axes):
    return lax.all_to_all(x, axes, 0, 0, tiled=True)


def body(gradient):
    height, width = gradient.shape
    count = width // BLOCK
    chunks = width // CHUNK
    group = ("yl", "x")
    square = [pltpu.VMEM((BLOCK, BLOCK), F32)] * 2
    whole = [pltpu.VMEM((chunks, height, CHUNK), F32), pltpu.SemaphoreType.DMA((chunks,))]

    left, right = pl.pallas_call(
        gram_kernel,
        out_shape=[shape(PACKED, LANES), shape(count, PACKED, LANES)],
        compiler_params=PARAMS,
        name="grams",
    )(gradient)
    right = swap(right, group)
    left = left + shift(left, "z", 4)
    right, left = lax.optimization_barrier((jnp.sum(right, axis=0), left))
    rest = swap(jnp.broadcast_to(right[None], (lax.axis_size("yh"),) + right.shape), "yh")
    left = left + shift(left, "core", 1)
    left = left + shift(left, "z", 1)
    other = shift(left, "z", 2)

    roots = pl.pallas_call(
        right_root_kernel,
        out_shape=shape(count, PACKED, LANES),
        scratch_shapes=square,
        compiler_params=PARAMS,
        name="right_root",
        cost_estimate=estimate(16 * 10**9),
    )(rest)
    roots, left, other = lax.optimization_barrier((roots, left, other))
    left = left + other
    received = swap(roots, group)

    high, low = pl.pallas_call(
        left_root_kernel,
        out_shape=[shape(count, height, BLOCK, dtype=BF16)] * 2,
        scratch_shapes=square,
        compiler_params=PARAMS,
        name="left_root",
        cost_estimate=estimate(8 * 10**9),
    )(left, gradient)
    return pl.pallas_call(
        update_kernel,
        out_specs=pl.BlockSpec(memory_space=pl.ANY),
        out_shape=shape(height, width),
        scratch_shapes=whole,
        compiler_params=PARAMS,
        name="update",
    )(high, low, received)


def solution(mesh):
    names = ("yh", "yl", "x", "z", "core")
    fine = Mesh(mesh.devices.reshape(4, 2, 4, 8, 2), names)
    spec = P(names[:3], names[3:])
    return jax.shard_map(body, mesh=fine, in_specs=(spec,), out_specs=spec, check_vma=False)
```

```python
import functools

import jax
import jax.numpy as jnp
from jax import lax
from jax.experimental import pallas as pl
from jax.experimental.pallas import tpu as pltpu
from jax.sharding import Mesh, PartitionSpec as P

D_IN = 6144
D_OUT = 24576
BLOCK = 192
ITERS = 12
HALF = 96
LANES = 128
PACKED = 152
CHUNK = 2 * BLOCK
SCALE = (float(D_IN) * float(D_OUT)) ** 0.25
F32, BF16 = jnp.float32, jnp.bfloat16
PARAMS = pltpu.CompilerParams(vmem_limit_bytes=32 * 2**20)


def split(a):
    high = a.astype(BF16)
    return high, (a - high.astype(F32)).astype(BF16)


def dot(a, b, dims=((1,), (0,))):
    return lax.dot_general(a, b, (dims, ((), ())), preferred_element_type=F32)


def product(a, b, dims=((1,), (0,))):
    return dot(a[0], b[0], dims) + (dot(a[0], b[1], dims) + dot(a[1], b[0], dims))


def grid_of(height, width):
    shape = (height, width)
    return lax.broadcasted_iota(jnp.int32, shape, 0), lax.broadcasted_iota(jnp.int32, shape, 1)


def pack(a):
    tail = a[HALF:, HALF:]
    row, col = grid_of(HALF, LANES)
    wide = jnp.concatenate([tail, jnp.zeros((HALF, LANES - HALF), F32)], axis=1)
    top = jnp.where(col < row, wide, a[:HALF, :LANES])
    rest = a[:HALF, LANES:]
    diagonal = jnp.sum(jnp.where(row == col, wide, 0.0), axis=0, keepdims=True)
    return jnp.concatenate(
        [
            top,
            jnp.concatenate([rest[: HALF // 2], rest[HALF // 2 :]], axis=1),
            jnp.broadcast_to(diagonal, (8, LANES)),
        ],
        axis=0,
    )


def unpack(p):
    row, col = grid_of(HALF, HALF)
    upper = p[:HALF, :HALF]
    lower = upper.T
    middle = p[HALF : HALF + HALF // 2]
    rest = jnp.concatenate(
        [p[:HALF, HALF:], jnp.concatenate([middle[:, :64], middle[:, 64:]], axis=0)], axis=1
    )
    head = jnp.where(col < row, lower, upper)
    tail = jnp.where(col < row, upper, jnp.where(col == row, p[144:145, :HALF], lower))
    return jnp.concatenate(
        [jnp.concatenate([head, rest], axis=1), jnp.concatenate([rest.T, tail], axis=1)], axis=0
    )


def gram_kernel(grad_ref, left_ref, right_ref):
    rows, columns = ((0,), (0,)), ((1,), (1,))
    left = None
    for k in range(grad_ref.shape[1] // CHUNK):
        g = split(grad_ref[:, k * CHUNK : (k + 1) * CHUNK])
        part = product(g, g, columns)
        left = part if k == 0 else left + part
        for c in range(CHUNK // BLOCK):
            h = [part[:, c * BLOCK : (c + 1) * BLOCK] for part in g]
            right_ref[k * (CHUNK // BLOCK) + c] = pack(product(h, h, rows))
    left_ref[...] = pack(left)


def newton(gram, m_ref, x_ref):
    row, col = grid_of(BLOCK, BLOCK)
    identity = (row == col).astype(F32)
    damped = gram + (0.01 / BLOCK * jnp.sum(gram * identity)) * identity
    norm = jnp.sqrt(jnp.sum(damped * damped, keepdims=True))
    m = damped / norm
    bands = [slice(0, HALF), slice(HALF, BLOCK)]

    def advance(m):
        parts = split(m)
        excess = [
            split(0.0625 * product((parts[0][b], parts[1][b]), parts) - 0.625 * m[b]) for b in bands
        ]
        halfway = [1.5625 * m[b] + product(e, parts) for e, b in zip(excess, bands)]
        whole = [jnp.concatenate([e[k] for e in excess], axis=0) for k in range(2)]
        return parts, jnp.concatenate([1.5625 * h + product(split(h), whole) for h in halfway], axis=0)

    def grow(parts):
        x = x_ref[...]
        return jnp.concatenate(
            [1.25 * x[b] - 0.25 * product(split(x[b]), parts) for b in bands], axis=0
        )

    x_ref[...] = (5.0 * identity - m) * 0.25
    m_ref[...] = advance(m)[1]

    def step(k, carry):
        parts, following = advance(m_ref[...])
        m_ref[...] = following
        x_ref[...] = grow(parts)
        return carry

    lax.fori_loop(0, ITERS - 2, step, 0, unroll=True)
    return grow(split(m_ref[...])) * lax.rsqrt(jnp.sqrt(norm))


def right_root_kernel(parts_ref, roots_ref, m_ref, x_ref):
    total = functools.reduce(lambda a, b: a + b, [parts_ref[k] for k in range(parts_ref.shape[0])])
    root = pack(newton(unpack(total), m_ref, x_ref))
    for k in range(roots_ref.shape[0]):
        roots_ref[k] = root


def left_root_kernel(gram_ref, grad_ref, high_ref, low_ref, m_ref, x_ref):
    root = split(newton(unpack(gram_ref[...]), m_ref, x_ref))
    for k in range(grad_ref.shape[1] // CHUNK):
        mid = split(product(root, split(grad_ref[:, k * CHUNK : (k + 1) * CHUNK])))
        for c in range(CHUNK // BLOCK):
            window = slice(c * BLOCK, (c + 1) * BLOCK)
            high_ref[2 * k + c] = mid[0][:, window]
            low_ref[2 * k + c] = mid[1][:, window]


def halves(p):
    row, col = grid_of(HALF, HALF)
    found = []
    for part in split(p):
        square = part[:HALF, :HALF]
        none = jnp.zeros_like(square)
        middle = part[HALF : HALF + HALF // 2]
        rest = jnp.concatenate(
            [part[:HALF, HALF:], jnp.concatenate([middle[:, :64], middle[:, 64:]], axis=0)], axis=1
        )
        below = jnp.where(col < row, square, none)
        diagonal = jnp.broadcast_to(part[144:145, :HALF], (HALF, HALF))
        for head, tail in (
            (jnp.where(col >= row, square, none), jnp.where(col == row, diagonal, below)),
            (jnp.where(col > row, square, none), below),
        ):
            top = jnp.concatenate([head, rest], axis=1)
            found.append(jnp.concatenate([top, jnp.concatenate([none, tail], axis=1)], axis=0))
    return (found[0], found[2]), (found[1], found[3])


def update_kernel(high_ref, low_ref, roots_ref, out_ref, held, sems):
    stores = []
    for k in range(out_ref.shape[1] // CHUNK):
        for c in range(CHUNK // BLOCK):
            b = 2 * k + c
            mid = (high_ref[b], low_ref[b])
            plain, flipped = halves(roots_ref[b])
            block = product(mid, plain) + product(mid, flipped, ((1,), (1,)))
            held[k, :, c * BLOCK : (c + 1) * BLOCK] = block * SCALE
        stores.append(
            pltpu.make_async_copy(held.at[k], out_ref.at[:, pl.ds(k * CHUNK, CHUNK)], sems.at[k])
        )
        stores[-1].start()
    for store in stores:
        store.wait()


def shape(*dims, dtype=F32):
    return jax.ShapeDtypeStruct(dims, dtype)


def estimate(flops):
    return pl.CostEstimate(flops=flops, bytes_accessed=2**20, transcendentals=0)


def shift(x, axis, by):
    n = lax.axis_size(axis)
    return lax.ppermute(x, axis, [(i, (i + by) % n) for i in range(n)])


def swap(x, axes):
    return lax.all_to_all(x, axes, 0, 0, tiled=True)


def body(gradient):
    height, width = gradient.shape
    count = width // BLOCK
    chunks = width // CHUNK
    group = ("yl", "x")
    square = [pltpu.VMEM((BLOCK, BLOCK), F32)] * 2
    whole = [pltpu.VMEM((chunks, height, CHUNK), F32), pltpu.SemaphoreType.DMA((chunks,))]

    left, right = pl.pallas_call(
        gram_kernel,
        out_shape=[shape(PACKED, LANES), shape(count, PACKED, LANES)],
        compiler_params=PARAMS,
        name="grams",
    )(gradient)
    right = swap(right, group)
    left = left + shift(left, "z", 4)
    right, left = lax.optimization_barrier((jnp.sum(right, axis=0), left))
    rest = swap(jnp.broadcast_to(right[None], (lax.axis_size("yh"),) + right.shape), "yh")
    left = left + shift(left, "core", 1)
    others = [shift(left, "z", by) for by in (1, 7, 2)]

    roots = pl.pallas_call(
        right_root_kernel,
        out_shape=shape(count, PACKED, LANES),
        scratch_shapes=square,
        compiler_params=PARAMS,
        name="right_root",
        cost_estimate=estimate(16 * 10**9),
    )(rest)
    roots, left, others = lax.optimization_barrier((roots, left, others))
    left = sum(others, left)
    received = swap(roots, group)

    high, low = pl.pallas_call(
        left_root_kernel,
        out_shape=[shape(count, height, BLOCK, dtype=BF16)] * 2,
        scratch_shapes=square,
        compiler_params=PARAMS,
        name="left_root",
        cost_estimate=estimate(8 * 10**9),
    )(left, gradient)
    return pl.pallas_call(
        update_kernel,
        out_specs=pl.BlockSpec(memory_space=pl.ANY),
        out_shape=shape(height, width),
        scratch_shapes=whole,
        compiler_params=PARAMS,
        name="update",
    )(high, low, received)


def solution(mesh):
    names = ("yh", "yl", "x", "z", "core")
    fine = Mesh(mesh.devices.reshape(4, 2, 4, 8, 2), names)
    spec = P(names[:3], names[3:])
    return jax.shard_map(body, mesh=fine, in_specs=(spec,), out_specs=spec, check_vma=False)
```

```python
import functools

import jax
import jax.numpy as jnp
from jax import lax
from jax.experimental import pallas as pl
from jax.experimental.pallas import tpu as pltpu
from jax.sharding import Mesh, PartitionSpec as P

D_IN = 6144
D_OUT = 24576
BLOCK = 192
ITERS = 12
HALF = 96
LANES = 128
PACKED = 152
CHUNK = 2 * BLOCK
SCALE = (float(D_IN) * float(D_OUT)) ** 0.25
F32, BF16 = jnp.float32, jnp.bfloat16
PARAMS = pltpu.CompilerParams(vmem_limit_bytes=32 * 2**20)


def split(a):
    high = a.astype(BF16)
    return high, (a - high.astype(F32)).astype(BF16)


def dot(a, b, dims=((1,), (0,))):
    return lax.dot_general(a, b, (dims, ((), ())), preferred_element_type=F32)


def product(a, b, dims=((1,), (0,))):
    return dot(a[0], b[0], dims) + (dot(a[0], b[1], dims) + dot(a[1], b[0], dims))


def grid_of(height, width):
    shape = (height, width)
    return lax.broadcasted_iota(jnp.int32, shape, 0), lax.broadcasted_iota(jnp.int32, shape, 1)


def pack(a):
    tail = a[HALF:, HALF:]
    row, col = grid_of(HALF, LANES)
    wide = jnp.concatenate([tail, jnp.zeros((HALF, LANES - HALF), F32)], axis=1)
    top = jnp.where(col < row, wide, a[:HALF, :LANES])
    rest = a[:HALF, LANES:]
    diagonal = jnp.sum(jnp.where(row == col, wide, 0.0), axis=0, keepdims=True)
    return jnp.concatenate(
        [
            top,
            jnp.concatenate([rest[: HALF // 2], rest[HALF // 2 :]], axis=1),
            jnp.broadcast_to(diagonal, (8, LANES)),
        ],
        axis=0,
    )


def unpack(p):
    row, col = grid_of(HALF, HALF)
    upper = p[:HALF, :HALF]
    lower = upper.T
    middle = p[HALF : HALF + HALF // 2]
    rest = jnp.concatenate(
        [p[:HALF, HALF:], jnp.concatenate([middle[:, :64], middle[:, 64:]], axis=0)], axis=1
    )
    head = jnp.where(col < row, lower, upper)
    tail = jnp.where(col < row, upper, jnp.where(col == row, p[144:145, :HALF], lower))
    return jnp.concatenate(
        [jnp.concatenate([head, rest], axis=1), jnp.concatenate([rest.T, tail], axis=1)], axis=0
    )


def gram_kernel(grad_ref, left_ref, right_ref):
    rows, columns = ((0,), (0,)), ((1,), (1,))
    left = None
    for k in range(grad_ref.shape[1] // CHUNK):
        g = split(grad_ref[:, k * CHUNK : (k + 1) * CHUNK])
        part = product(g, g, columns)
        left = part if k == 0 else left + part
        for c in range(CHUNK // BLOCK):
            h = [part[:, c * BLOCK : (c + 1) * BLOCK] for part in g]
            right_ref[k * (CHUNK // BLOCK) + c] = pack(product(h, h, rows))
    left_ref[...] = pack(left)


def newton(gram, m_ref, x_ref):
    row, col = grid_of(BLOCK, BLOCK)
    identity = (row == col).astype(F32)
    damped = gram + (0.01 / BLOCK * jnp.sum(gram * identity)) * identity
    norm = jnp.sqrt(jnp.sum(damped * damped, keepdims=True))
    m = damped / norm
    bands = [slice(0, HALF), slice(HALF, BLOCK)]

    def advance(m):
        parts = split(m)
        excess = [
            split(0.0625 * product((parts[0][b], parts[1][b]), parts) - 0.625 * m[b]) for b in bands
        ]
        halfway = [1.5625 * m[b] + product(e, parts) for e, b in zip(excess, bands)]
        whole = [jnp.concatenate([e[k] for e in excess], axis=0) for k in range(2)]
        return parts, jnp.concatenate([1.5625 * h + product(split(h), whole) for h in halfway], axis=0)

    def grow(parts):
        x = x_ref[...]
        return jnp.concatenate(
            [1.25 * x[b] - 0.25 * product(split(x[b]), parts) for b in bands], axis=0
        )

    x_ref[...] = (5.0 * identity - m) * 0.25
    m_ref[...] = advance(m)[1]

    def step(k, carry):
        parts, following = advance(m_ref[...])
        m_ref[...] = following
        x_ref[...] = grow(parts)
        return carry

    lax.fori_loop(0, ITERS - 2, step, 0, unroll=True)
    return grow(split(m_ref[...])) * lax.rsqrt(jnp.sqrt(norm))


def right_root_kernel(parts_ref, roots_ref, m_ref, x_ref):
    total = functools.reduce(lambda a, b: a + b, [parts_ref[k] for k in range(parts_ref.shape[0])])
    root = pack(newton(unpack(total), m_ref, x_ref))
    for k in range(roots_ref.shape[0]):
        roots_ref[k] = root


def left_root_kernel(gram_ref, grad_ref, high_ref, low_ref, m_ref, x_ref):
    root = split(newton(unpack(gram_ref[...]), m_ref, x_ref))
    for k in range(grad_ref.shape[1] // CHUNK):
        mid = split(product(root, split(grad_ref[:, k * CHUNK : (k + 1) * CHUNK])))
        for c in range(CHUNK // BLOCK):
            window = slice(c * BLOCK, (c + 1) * BLOCK)
            high_ref[2 * k + c] = mid[0][:, window]
            low_ref[2 * k + c] = mid[1][:, window]


def halves(p):
    row, col = grid_of(HALF, HALF)
    found = []
    for part in split(p):
        square = part[:HALF, :HALF]
        none = jnp.zeros_like(square)
        middle = part[HALF : HALF + HALF // 2]
        rest = jnp.concatenate(
            [part[:HALF, HALF:], jnp.concatenate([middle[:, :64], middle[:, 64:]], axis=0)], axis=1
        )
        below = jnp.where(col < row, square, none)
        diagonal = jnp.broadcast_to(part[144:145, :HALF], (HALF, HALF))
        for head, tail in (
            (jnp.where(col >= row, square, none), jnp.where(col == row, diagonal, below)),
            (jnp.where(col > row, square, none), below),
        ):
            top = jnp.concatenate([head, rest], axis=1)
            found.append(jnp.concatenate([top, jnp.concatenate([none, tail], axis=1)], axis=0))
    return (found[0], found[2]), (found[1], found[3])


def update_kernel(high_ref, low_ref, roots_ref, out_ref, held, sems):
    stores = []
    for k in range(out_ref.shape[1] // CHUNK):
        for c in range(CHUNK // BLOCK):
            b = 2 * k + c
            mid = (high_ref[b], low_ref[b])
            plain, flipped = halves(roots_ref[b])
            block = product(mid, plain) + product(mid, flipped, ((1,), (1,)))
            held[k, :, c * BLOCK : (c + 1) * BLOCK] = block * SCALE
        stores.append(
            pltpu.make_async_copy(held.at[k], out_ref.at[:, pl.ds(k * CHUNK, CHUNK)], sems.at[k])
        )
        stores[-1].start()
    for store in stores:
        store.wait()


def shape(*dims, dtype=F32):
    return jax.ShapeDtypeStruct(dims, dtype)


def estimate(flops):
    return pl.CostEstimate(flops=flops, bytes_accessed=2**20, transcendentals=0)


def shift(x, axis, by):
    n = lax.axis_size(axis)
    return lax.ppermute(x, axis, [(i, (i + by) % n) for i in range(n)])


def other_of_pair(x, axis):
    return lax.ppermute(x, axis, [(i, i ^ 1) for i in range(lax.axis_size(axis))])


def swap(x, axes):
    return lax.all_to_all(x, axes, 0, 0, tiled=True)


def body(gradient):
    height, width = gradient.shape
    count = width // BLOCK
    chunks = width // CHUNK
    group = ("yl", "x")
    square = [pltpu.VMEM((BLOCK, BLOCK), F32)] * 2
    whole = [pltpu.VMEM((chunks, height, CHUNK), F32), pltpu.SemaphoreType.DMA((chunks,))]

    left, right = pl.pallas_call(
        gram_kernel,
        out_shape=[shape(PACKED, LANES), shape(count, PACKED, LANES)],
        compiler_params=PARAMS,
        name="grams",
    )(gradient)
    right = swap(right, group)
    left = left + other_of_pair(left, "core")
    left = left + other_of_pair(left, "z")
    right, left = lax.optimization_barrier((jnp.sum(right, axis=0), left))
    rest = swap(jnp.broadcast_to(right[None], (lax.axis_size("yh"),) + right.shape), "yh")
    others = [shift(left, "z", by) for by in (2, 6, 4)]

    roots = pl.pallas_call(
        right_root_kernel,
        out_shape=shape(count, PACKED, LANES),
        scratch_shapes=square,
        compiler_params=PARAMS,
        name="right_root",
        cost_estimate=estimate(16 * 10**9),
    )(rest)
    roots, left, others = lax.optimization_barrier((roots, left, others))
    left = sum(others, left)
    received = swap(roots, group)

    high, low = pl.pallas_call(
        left_root_kernel,
        out_shape=[shape(count, height, BLOCK, dtype=BF16)] * 2,
        scratch_shapes=square,
        compiler_params=PARAMS,
        name="left_root",
        cost_estimate=estimate(8 * 10**9),
    )(left, gradient)
    return pl.pallas_call(
        update_kernel,
        out_specs=pl.BlockSpec(memory_space=pl.ANY),
        out_shape=shape(height, width),
        scratch_shapes=whole,
        compiler_params=PARAMS,
        name="update",
    )(high, low, received)


def solution(mesh):
    names = ("yh", "yl", "x", "z", "core")
    fine = Mesh(mesh.devices.reshape(4, 2, 4, 8, 2), names)
    spec = P(names[:3], names[3:])
    return jax.shard_map(body, mesh=fine, in_specs=(spec,), out_specs=spec, check_vma=False)
```

```python
import functools

import jax
import jax.numpy as jnp
from jax import lax
from jax.experimental import pallas as pl
from jax.experimental.pallas import tpu as pltpu
from jax.sharding import Mesh, PartitionSpec as P

D_IN = 6144
D_OUT = 24576
BLOCK = 192
ITERS = 12
HALF = 96
LANES = 128
PACKED = 152
CHUNK = 2 * BLOCK
SCALE = (float(D_IN) * float(D_OUT)) ** 0.25
F32, BF16 = jnp.float32, jnp.bfloat16
PARAMS = pltpu.CompilerParams(vmem_limit_bytes=32 * 2**20)


def split(a):
    high = a.astype(BF16)
    return high, (a - high.astype(F32)).astype(BF16)


def dot(a, b, dims=((1,), (0,))):
    return lax.dot_general(a, b, (dims, ((), ())), preferred_element_type=F32)


def product(a, b, dims=((1,), (0,))):
    return dot(a[0], b[0], dims) + (dot(a[0], b[1], dims) + dot(a[1], b[0], dims))


def grid_of(height, width):
    shape = (height, width)
    return lax.broadcasted_iota(jnp.int32, shape, 0), lax.broadcasted_iota(jnp.int32, shape, 1)


def pack(a):
    tail = a[HALF:, HALF:]
    row, col = grid_of(HALF, LANES)
    wide = jnp.concatenate([tail, jnp.zeros((HALF, LANES - HALF), F32)], axis=1)
    top = jnp.where(col < row, wide, a[:HALF, :LANES])
    rest = a[:HALF, LANES:]
    diagonal = jnp.sum(jnp.where(row == col, wide, 0.0), axis=0, keepdims=True)
    return jnp.concatenate(
        [
            top,
            jnp.concatenate([rest[: HALF // 2], rest[HALF // 2 :]], axis=1),
            jnp.broadcast_to(diagonal, (8, LANES)),
        ],
        axis=0,
    )


def unpack(p):
    row, col = grid_of(HALF, HALF)
    upper = p[:HALF, :HALF]
    lower = upper.T
    middle = p[HALF : HALF + HALF // 2]
    rest = jnp.concatenate(
        [p[:HALF, HALF:], jnp.concatenate([middle[:, :64], middle[:, 64:]], axis=0)], axis=1
    )
    head = jnp.where(col < row, lower, upper)
    tail = jnp.where(col < row, upper, jnp.where(col == row, p[144:145, :HALF], lower))
    return jnp.concatenate(
        [jnp.concatenate([head, rest], axis=1), jnp.concatenate([rest.T, tail], axis=1)], axis=0
    )


def gram_kernel(grad_ref, left_ref, right_ref):
    rows, columns = ((0,), (0,)), ((1,), (1,))
    left = None
    for k in range(grad_ref.shape[1] // CHUNK):
        g = split(grad_ref[:, k * CHUNK : (k + 1) * CHUNK])
        part = product(g, g, columns)
        left = part if k == 0 else left + part
        for c in range(CHUNK // BLOCK):
            h = [part[:, c * BLOCK : (c + 1) * BLOCK] for part in g]
            right_ref[k * (CHUNK // BLOCK) + c] = pack(product(h, h, rows))
    left_ref[...] = pack(left)


def newton(gram, m_ref, x_ref):
    row, col = grid_of(BLOCK, BLOCK)
    identity = (row == col).astype(F32)
    damped = gram + (0.01 / BLOCK * jnp.sum(gram * identity)) * identity
    norm = jnp.sqrt(jnp.sum(damped * damped, keepdims=True))
    m = damped / norm
    bands = [slice(0, HALF), slice(HALF, BLOCK)]

    def advance(m):
        parts = split(m)
        excess = [
            split(0.0625 * product((parts[0][b], parts[1][b]), parts) - 0.625 * m[b]) for b in bands
        ]
        halfway = [1.5625 * m[b] + product(e, parts) for e, b in zip(excess, bands)]
        whole = [jnp.concatenate([e[k] for e in excess], axis=0) for k in range(2)]
        return parts, jnp.concatenate([1.5625 * h + product(split(h), whole) for h in halfway], axis=0)

    def grow(parts):
        x = x_ref[...]
        return jnp.concatenate(
            [1.25 * x[b] - 0.25 * product(split(x[b]), parts) for b in bands], axis=0
        )

    x_ref[...] = (5.0 * identity - m) * 0.25
    m_ref[...] = advance(m)[1]

    def step(k, carry):
        parts, following = advance(m_ref[...])
        m_ref[...] = following
        x_ref[...] = grow(parts)
        return carry

    lax.fori_loop(0, ITERS - 2, step, 0, unroll=True)
    return grow(split(m_ref[...])) * lax.rsqrt(jnp.sqrt(norm))


def right_root_kernel(parts_ref, roots_ref, m_ref, x_ref):
    total = functools.reduce(lambda a, b: a + b, [parts_ref[k] for k in range(parts_ref.shape[0])])
    root = pack(newton(unpack(total), m_ref, x_ref))
    for k in range(roots_ref.shape[0]):
        roots_ref[k] = root


def left_root_kernel(gram_ref, grad_ref, high_ref, low_ref, m_ref, x_ref):
    root = split(newton(unpack(gram_ref[...]), m_ref, x_ref))
    for k in range(grad_ref.shape[1] // CHUNK):
        mid = split(product(root, split(grad_ref[:, k * CHUNK : (k + 1) * CHUNK])))
        for c in range(CHUNK // BLOCK):
            window = slice(c * BLOCK, (c + 1) * BLOCK)
            high_ref[2 * k + c] = mid[0][:, window]
            low_ref[2 * k + c] = mid[1][:, window]


def halves(p):
    row, col = grid_of(HALF, HALF)
    found = []
    for part in split(p):
        square = part[:HALF, :HALF]
        none = jnp.zeros_like(square)
        middle = part[HALF : HALF + HALF // 2]
        rest = jnp.concatenate(
            [part[:HALF, HALF:], jnp.concatenate([middle[:, :64], middle[:, 64:]], axis=0)], axis=1
        )
        below = jnp.where(col < row, square, none)
        diagonal = jnp.broadcast_to(part[144:145, :HALF], (HALF, HALF))
        for head, tail in (
            (jnp.where(col >= row, square, none), jnp.where(col == row, diagonal, below)),
            (jnp.where(col > row, square, none), below),
        ):
            top = jnp.concatenate([head, rest], axis=1)
            found.append(jnp.concatenate([top, jnp.concatenate([none, tail], axis=1)], axis=0))
    return (found[0], found[2]), (found[1], found[3])


def update_kernel(high_ref, low_ref, roots_ref, out_ref, held, sems):
    stores = []
    for k in range(out_ref.shape[1] // CHUNK):
        for c in range(CHUNK // BLOCK):
            b = 2 * k + c
            mid = (high_ref[b], low_ref[b])
            plain, flipped = halves(roots_ref[b])
            block = product(mid, plain) + product(mid, flipped, ((1,), (1,)))
            held[k, :, c * BLOCK : (c + 1) * BLOCK] = block * SCALE
        stores.append(
            pltpu.make_async_copy(held.at[k], out_ref.at[:, pl.ds(k * CHUNK, CHUNK)], sems.at[k])
        )
        stores[-1].start()
    for store in stores:
        store.wait()


def shape(*dims, dtype=F32):
    return jax.ShapeDtypeStruct(dims, dtype)


def estimate(flops):
    return pl.CostEstimate(flops=flops, bytes_accessed=2**20, transcendentals=0)


def shift(x, axis, by):
    n = lax.axis_size(axis)
    return lax.ppermute(x, axis, [(i, (i + by) % n) for i in range(n)])


def other_of_pair(x, axis):
    return lax.ppermute(x, axis, [(i, i ^ 1) for i in range(lax.axis_size(axis))])


def swap(x, axes):
    return lax.all_to_all(x, axes, 0, 0, tiled=True)


def body(gradient):
    height, width = gradient.shape
    count = width // BLOCK
    chunks = width // CHUNK
    group = ("yl", "x")
    square = [pltpu.VMEM((BLOCK, BLOCK), F32)] * 2
    whole = [pltpu.VMEM((chunks, height, CHUNK), F32), pltpu.SemaphoreType.DMA((chunks,))]

    left, right = pl.pallas_call(
        gram_kernel,
        out_shape=[shape(PACKED, LANES), shape(count, PACKED, LANES)],
        compiler_params=PARAMS,
        name="grams",
    )(gradient)
    right = swap(right, group)
    left = left + other_of_pair(left, "core")
    left = left + other_of_pair(left, "z")
    right, left = lax.optimization_barrier((jnp.sum(right, axis=0), left))
    rest = swap(jnp.broadcast_to(right[None], (lax.axis_size("yh"),) + right.shape), "yh")
    others = [shift(left, "z", by) for by in (4, 6, 2)]

    roots = pl.pallas_call(
        right_root_kernel,
        out_shape=shape(count, PACKED, LANES),
        scratch_shapes=square,
        compiler_params=PARAMS,
        name="right_root",
        cost_estimate=estimate(16 * 10**9),
    )(rest)
    roots, left, others = lax.optimization_barrier((roots, left, others))
    left = sum(others, left)
    received = swap(roots, group)

    high, low = pl.pallas_call(
        left_root_kernel,
        out_shape=[shape(count, height, BLOCK, dtype=BF16)] * 2,
        scratch_shapes=square,
        compiler_params=PARAMS,
        name="left_root",
        cost_estimate=estimate(8 * 10**9),
    )(left, gradient)
    return pl.pallas_call(
        update_kernel,
        out_specs=pl.BlockSpec(memory_space=pl.ANY),
        out_shape=shape(height, width),
        scratch_shapes=whole,
        compiler_params=PARAMS,
        name="update",
    )(high, low, received)


def solution(mesh):
    names = ("yh", "yl", "x", "z", "core")
    fine = Mesh(mesh.devices.reshape(4, 2, 4, 8, 2), names)
    spec = P(names[:3], names[3:])
    return jax.shard_map(body, mesh=fine, in_specs=(spec,), out_specs=spec, check_vma=False)
```

```python
import functools

import jax
import jax.numpy as jnp
from jax import lax
from jax.experimental import pallas as pl
from jax.experimental.pallas import tpu as pltpu
from jax.sharding import Mesh, PartitionSpec as P

D_IN = 6144
D_OUT = 24576
BLOCK = 192
ITERS = 12
HALF = 96
LANES = 128
PACKED = 152
CHUNK = 2 * BLOCK
SCALE = (float(D_IN) * float(D_OUT)) ** 0.25
F32, BF16 = jnp.float32, jnp.bfloat16
PARAMS = pltpu.CompilerParams(vmem_limit_bytes=32 * 2**20)


def split(a):
    high = a.astype(BF16)
    return high, (a - high.astype(F32)).astype(BF16)


def dot(a, b, dims=((1,), (0,))):
    return lax.dot_general(a, b, (dims, ((), ())), preferred_element_type=F32)


def product(a, b, dims=((1,), (0,))):
    return dot(a[0], b[0], dims) + (dot(a[0], b[1], dims) + dot(a[1], b[0], dims))


def grid_of(height, width):
    shape = (height, width)
    return lax.broadcasted_iota(jnp.int32, shape, 0), lax.broadcasted_iota(jnp.int32, shape, 1)


def pack(a):
    tail = a[HALF:, HALF:]
    row, col = grid_of(HALF, LANES)
    wide = jnp.concatenate([tail, jnp.zeros((HALF, LANES - HALF), F32)], axis=1)
    top = jnp.where(col < row, wide, a[:HALF, :LANES])
    rest = a[:HALF, LANES:]
    diagonal = jnp.sum(jnp.where(row == col, wide, 0.0), axis=0, keepdims=True)
    return jnp.concatenate(
        [
            top,
            jnp.concatenate([rest[: HALF // 2], rest[HALF // 2 :]], axis=1),
            jnp.broadcast_to(diagonal, (8, LANES)),
        ],
        axis=0,
    )


def unpack(p):
    row, col = grid_of(HALF, HALF)
    upper = p[:HALF, :HALF]
    lower = upper.T
    middle = p[HALF : HALF + HALF // 2]
    rest = jnp.concatenate(
        [p[:HALF, HALF:], jnp.concatenate([middle[:, :64], middle[:, 64:]], axis=0)], axis=1
    )
    head = jnp.where(col < row, lower, upper)
    tail = jnp.where(col < row, upper, jnp.where(col == row, p[144:145, :HALF], lower))
    return jnp.concatenate(
        [jnp.concatenate([head, rest], axis=1), jnp.concatenate([rest.T, tail], axis=1)], axis=0
    )


def gram_kernel(grad_ref, left_ref, right_ref):
    rows, columns = ((0,), (0,)), ((1,), (1,))
    left = None
    for k in range(grad_ref.shape[1] // CHUNK):
        g = split(grad_ref[:, k * CHUNK : (k + 1) * CHUNK])
        part = product(g, g, columns)
        left = part if k == 0 else left + part
        for c in range(CHUNK // BLOCK):
            h = [part[:, c * BLOCK : (c + 1) * BLOCK] for part in g]
            right_ref[k * (CHUNK // BLOCK) + c] = pack(product(h, h, rows))
    left_ref[...] = pack(left)


def newton(gram, m_ref, x_ref):
    row, col = grid_of(BLOCK, BLOCK)
    identity = (row == col).astype(F32)
    damped = gram + (0.01 / BLOCK * jnp.sum(gram * identity)) * identity
    norm = jnp.sqrt(jnp.sum(damped * damped, keepdims=True))
    m = damped / norm
    bands = [slice(0, HALF), slice(HALF, BLOCK)]

    def advance(m):
        parts = split(m)
        excess = [
            split(0.0625 * product((parts[0][b], parts[1][b]), parts) - 0.625 * m[b]) for b in bands
        ]
        halfway = [1.5625 * m[b] + product(e, parts) for e, b in zip(excess, bands)]
        whole = [jnp.concatenate([e[k] for e in excess], axis=0) for k in range(2)]
        return parts, jnp.concatenate([1.5625 * h + product(split(h), whole) for h in halfway], axis=0)

    def grow(parts):
        x = x_ref[...]
        return jnp.concatenate(
            [1.25 * x[b] - 0.25 * product(split(x[b]), parts) for b in bands], axis=0
        )

    x_ref[...] = (5.0 * identity - m) * 0.25
    m_ref[...] = advance(m)[1]

    def step(k, carry):
        parts, following = advance(m_ref[...])
        m_ref[...] = following
        x_ref[...] = grow(parts)
        return carry

    lax.fori_loop(0, ITERS - 2, step, 0, unroll=True)
    return grow(split(m_ref[...])) * lax.rsqrt(jnp.sqrt(norm))


def right_root_kernel(parts_ref, roots_ref, m_ref, x_ref):
    total = functools.reduce(lambda a, b: a + b, [parts_ref[k] for k in range(parts_ref.shape[0])])
    root = pack(newton(unpack(total), m_ref, x_ref))
    for k in range(roots_ref.shape[0]):
        roots_ref[k] = root


def left_root_kernel(gram_ref, grad_ref, high_ref, low_ref, m_ref, x_ref):
    root = split(newton(unpack(gram_ref[...]), m_ref, x_ref))
    for k in range(grad_ref.shape[1] // CHUNK):
        mid = split(product(root, split(grad_ref[:, k * CHUNK : (k + 1) * CHUNK])))
        for c in range(CHUNK // BLOCK):
            window = slice(c * BLOCK, (c + 1) * BLOCK)
            high_ref[2 * k + c] = mid[0][:, window]
            low_ref[2 * k + c] = mid[1][:, window]


def halves(p):
    row, col = grid_of(HALF, HALF)
    found = []
    for part in split(p):
        square = part[:HALF, :HALF]
        none = jnp.zeros_like(square)
        middle = part[HALF : HALF + HALF // 2]
        rest = jnp.concatenate(
            [part[:HALF, HALF:], jnp.concatenate([middle[:, :64], middle[:, 64:]], axis=0)], axis=1
        )
        below = jnp.where(col < row, square, none)
        diagonal = jnp.broadcast_to(part[144:145, :HALF], (HALF, HALF))
        for head, tail in (
            (jnp.where(col >= row, square, none), jnp.where(col == row, diagonal, below)),
            (jnp.where(col > row, square, none), below),
        ):
            top = jnp.concatenate([head, rest], axis=1)
            found.append(jnp.concatenate([top, jnp.concatenate([none, tail], axis=1)], axis=0))
    return (found[0], found[2]), (found[1], found[3])


def update_kernel(high_ref, low_ref, roots_ref, out_ref, held, sems):
    stores = []
    for k in range(out_ref.shape[1] // CHUNK):
        for c in range(CHUNK // BLOCK):
            b = 2 * k + c
            mid = (high_ref[b], low_ref[b])
            plain, flipped = halves(roots_ref[b])
            block = product(mid, plain) + product(mid, flipped, ((1,), (1,)))
            held[k, :, c * BLOCK : (c + 1) * BLOCK] = block * SCALE
        stores.append(
            pltpu.make_async_copy(held.at[k], out_ref.at[:, pl.ds(k * CHUNK, CHUNK)], sems.at[k])
        )
        stores[-1].start()
    for store in stores:
        store.wait()


def shape(*dims, dtype=F32):
    return jax.ShapeDtypeStruct(dims, dtype)


def estimate(flops):
    return pl.CostEstimate(flops=flops, bytes_accessed=2**20, transcendentals=0)


def partner(x, axis, bits):
    return lax.ppermute(x, axis, [(i, i ^ bits) for i in range(lax.axis_size(axis))])


def swap(x, axes):
    return lax.all_to_all(x, axes, 0, 0, tiled=True)


def body(gradient):
    height, width = gradient.shape
    count = width // BLOCK
    chunks = width // CHUNK
    group = ("yl", "x")
    square = [pltpu.VMEM((BLOCK, BLOCK), F32)] * 2
    whole = [pltpu.VMEM((chunks, height, CHUNK), F32), pltpu.SemaphoreType.DMA((chunks,))]

    left, right = pl.pallas_call(
        gram_kernel,
        out_shape=[shape(PACKED, LANES), shape(count, PACKED, LANES)],
        compiler_params=PARAMS,
        name="grams",
    )(gradient)
    right = swap(right, group)
    left = left + partner(left, "core", 1)
    left = left + partner(left, "z", 1)
    right, left = lax.optimization_barrier((jnp.sum(right, axis=0), left))
    rest = swap(jnp.broadcast_to(right[None], (lax.axis_size("yh"),) + right.shape), "yh")
    others = [partner(left, "z", bits) for bits in (2, 6, 4)]

    roots = pl.pallas_call(
        right_root_kernel,
        out_shape=shape(count, PACKED, LANES),
        scratch_shapes=square,
        compiler_params=PARAMS,
        name="right_root",
        cost_estimate=estimate(16 * 10**9),
    )(rest)
    roots, left, others = lax.optimization_barrier((roots, left, others))
    left = sum(others, left)
    received = swap(roots, group)

    high, low = pl.pallas_call(
        left_root_kernel,
        out_shape=[shape(count, height, BLOCK, dtype=BF16)] * 2,
        scratch_shapes=square,
        compiler_params=PARAMS,
        name="left_root",
        cost_estimate=estimate(8 * 10**9),
    )(left, gradient)
    return pl.pallas_call(
        update_kernel,
        out_specs=pl.BlockSpec(memory_space=pl.ANY),
        out_shape=shape(height, width),
        scratch_shapes=whole,
        compiler_params=PARAMS,
        name="update",
    )(high, low, received)


def solution(mesh):
    names = ("yh", "yl", "x", "z", "core")
    fine = Mesh(mesh.devices.reshape(4, 2, 4, 8, 2), names)
    spec = P(names[:3], names[3:])
    return jax.shard_map(body, mesh=fine, in_specs=(spec,), out_specs=spec, check_vma=False)
```

```python
import functools

import jax
import jax.numpy as jnp
from jax import lax
from jax.experimental import pallas as pl
from jax.experimental.pallas import tpu as pltpu
from jax.sharding import Mesh, PartitionSpec as P

D_IN = 6144
D_OUT = 24576
BLOCK = 192
ITERS = 12
HALF = 96
LANES = 128
PACKED = 152
CHUNK = 2 * BLOCK
SCALE = (float(D_IN) * float(D_OUT)) ** 0.25
F32, BF16 = jnp.float32, jnp.bfloat16
PARAMS = pltpu.CompilerParams(vmem_limit_bytes=32 * 2**20)


def split(a):
    high = a.astype(BF16)
    return high, (a - high.astype(F32)).astype(BF16)


def dot(a, b, dims=((1,), (0,))):
    return lax.dot_general(a, b, (dims, ((), ())), preferred_element_type=F32)


def product(a, b, dims=((1,), (0,))):
    return dot(a[0], b[0], dims) + (dot(a[0], b[1], dims) + dot(a[1], b[0], dims))


def grid_of(height, width):
    shape = (height, width)
    return lax.broadcasted_iota(jnp.int32, shape, 0), lax.broadcasted_iota(jnp.int32, shape, 1)


def pack(a):
    tail = a[HALF:, HALF:]
    row, col = grid_of(HALF, LANES)
    wide = jnp.concatenate([tail, jnp.zeros((HALF, LANES - HALF), F32)], axis=1)
    top = jnp.where(col < row, wide, a[:HALF, :LANES])
    rest = a[:HALF, LANES:]
    diagonal = jnp.sum(jnp.where(row == col, wide, 0.0), axis=0, keepdims=True)
    return jnp.concatenate(
        [
            top,
            jnp.concatenate([rest[: HALF // 2], rest[HALF // 2 :]], axis=1),
            jnp.broadcast_to(diagonal, (8, LANES)),
        ],
        axis=0,
    )


def unpack(p):
    row, col = grid_of(HALF, HALF)
    upper = p[:HALF, :HALF]
    lower = upper.T
    middle = p[HALF : HALF + HALF // 2]
    rest = jnp.concatenate(
        [p[:HALF, HALF:], jnp.concatenate([middle[:, :64], middle[:, 64:]], axis=0)], axis=1
    )
    head = jnp.where(col < row, lower, upper)
    tail = jnp.where(col < row, upper, jnp.where(col == row, p[144:145, :HALF], lower))
    return jnp.concatenate(
        [jnp.concatenate([head, rest], axis=1), jnp.concatenate([rest.T, tail], axis=1)], axis=0
    )


def gram_kernel(grad_ref, left_ref, right_ref):
    rows, columns = ((0,), (0,)), ((1,), (1,))
    left = None
    for k in range(grad_ref.shape[1] // CHUNK):
        g = split(grad_ref[:, k * CHUNK : (k + 1) * CHUNK])
        part = product(g, g, columns)
        left = part if k == 0 else left + part
        for c in range(CHUNK // BLOCK):
            h = [part[:, c * BLOCK : (c + 1) * BLOCK] for part in g]
            right_ref[k * (CHUNK // BLOCK) + c] = pack(product(h, h, rows))
    left_ref[...] = pack(left)


def newton(gram, m_ref, x_ref):
    row, col = grid_of(BLOCK, BLOCK)
    identity = (row == col).astype(F32)
    damped = gram + (0.01 / BLOCK * jnp.sum(gram * identity)) * identity
    norm = jnp.sqrt(jnp.sum(damped * damped, keepdims=True))
    m = damped / norm
    bands = [slice(0, HALF), slice(HALF, BLOCK)]

    def advance(m):
        parts = split(m)
        centred = (m - 0.5 * identity).astype(BF16)
        excess = [
            split(0.0625 * dot(centred[b], centred) - 0.015625 * identity[b] - 0.5625 * m[b])
            for b in bands
        ]
        halfway = [1.5625 * m[b] + product(e, parts) for e, b in zip(excess, bands)]
        whole = [jnp.concatenate([e[k] for e in excess], axis=0) for k in range(2)]
        return parts, jnp.concatenate([1.5625 * h + product(split(h), whole) for h in halfway], axis=0)

    def grow(parts):
        x = x_ref[...]
        return jnp.concatenate(
            [1.25 * x[b] - 0.25 * product(split(x[b]), parts) for b in bands], axis=0
        )

    x_ref[...] = (5.0 * identity - m) * 0.25
    m_ref[...] = advance(m)[1]

    def step(k, carry):
        parts, following = advance(m_ref[...])
        grown = grow(parts)
        m_ref[...] = following
        x_ref[...] = grown
        return carry

    lax.fori_loop(0, ITERS - 2, step, 0, unroll=True)
    return grow(split(m_ref[...])) * lax.rsqrt(jnp.sqrt(norm))


def right_root_kernel(parts_ref, roots_ref, m_ref, x_ref):
    total = functools.reduce(lambda a, b: a + b, [parts_ref[k] for k in range(parts_ref.shape[0])])
    root = pack(newton(unpack(total), m_ref, x_ref))
    for k in range(roots_ref.shape[0]):
        roots_ref[k] = root


def left_root_kernel(gram_ref, grad_ref, high_ref, low_ref, m_ref, x_ref):
    root = split(newton(unpack(gram_ref[...]), m_ref, x_ref))
    for k in range(grad_ref.shape[1] // CHUNK):
        mid = split(product(root, split(grad_ref[:, k * CHUNK : (k + 1) * CHUNK])))
        for c in range(CHUNK // BLOCK):
            window = slice(c * BLOCK, (c + 1) * BLOCK)
            high_ref[2 * k + c] = mid[0][:, window]
            low_ref[2 * k + c] = mid[1][:, window]


def halves(p):
    row, col = grid_of(HALF, HALF)
    found = []
    for part in split(p):
        square = part[:HALF, :HALF]
        none = jnp.zeros_like(square)
        middle = part[HALF : HALF + HALF // 2]
        rest = jnp.concatenate(
            [part[:HALF, HALF:], jnp.concatenate([middle[:, :64], middle[:, 64:]], axis=0)], axis=1
        )
        below = jnp.where(col < row, square, none)
        diagonal = jnp.broadcast_to(part[144:145, :HALF], (HALF, HALF))
        for head, tail in (
            (jnp.where(col >= row, square, none), jnp.where(col == row, diagonal, below)),
            (jnp.where(col > row, square, none), below),
        ):
            top = jnp.concatenate([head, rest], axis=1)
            found.append(jnp.concatenate([top, jnp.concatenate([none, tail], axis=1)], axis=0))
    return (found[0], found[2]), (found[1], found[3])


def update_kernel(high_ref, low_ref, roots_ref, out_ref, held, sems):
    stores = []
    for k in range(out_ref.shape[1] // CHUNK):
        for c in range(CHUNK // BLOCK):
            b = 2 * k + c
            mid = (high_ref[b], low_ref[b])
            plain, flipped = halves(roots_ref[b])
            block = product(mid, plain) + product(mid, flipped, ((1,), (1,)))
            held[k, :, c * BLOCK : (c + 1) * BLOCK] = block * SCALE
        stores.append(
            pltpu.make_async_copy(held.at[k], out_ref.at[:, pl.ds(k * CHUNK, CHUNK)], sems.at[k])
        )
        stores[-1].start()
    for store in stores:
        store.wait()


def shape(*dims, dtype=F32):
    return jax.ShapeDtypeStruct(dims, dtype)


def estimate(flops):
    return pl.CostEstimate(flops=flops, bytes_accessed=2**20, transcendentals=0)


def partner(x, axis, bits):
    return lax.ppermute(x, axis, [(i, i ^ bits) for i in range(lax.axis_size(axis))])


def swap(x, axes):
    return lax.all_to_all(x, axes, 0, 0, tiled=True)


def body(gradient):
    height, width = gradient.shape
    count = width // BLOCK
    chunks = width // CHUNK
    group = ("yl", "x")
    square = [pltpu.VMEM((BLOCK, BLOCK), F32)] * 2
    whole = [pltpu.VMEM((chunks, height, CHUNK), F32), pltpu.SemaphoreType.DMA((chunks,))]

    left, right = pl.pallas_call(
        gram_kernel,
        out_shape=[shape(PACKED, LANES), shape(count, PACKED, LANES)],
        compiler_params=PARAMS,
        name="grams",
    )(gradient)
    right = swap(right, group)
    left = left + partner(left, "core", 1)
    left = left + partner(left, "z", 1)
    right, left = lax.optimization_barrier((jnp.sum(right, axis=0), left))
    rest = swap(jnp.broadcast_to(right[None], (lax.axis_size("yh"),) + right.shape), "yh")
    others = [partner(left, "z", bits) for bits in (2, 6, 4)]

    roots = pl.pallas_call(
        right_root_kernel,
        out_shape=shape(count, PACKED, LANES),
        scratch_shapes=square,
        compiler_params=PARAMS,
        name="right_root",
        cost_estimate=estimate(16 * 10**9),
    )(rest)
    roots, left, others = lax.optimization_barrier((roots, left, others))
    left = sum(others, left)
    received = swap(roots, group)

    high, low = pl.pallas_call(
        left_root_kernel,
        out_shape=[shape(count, height, BLOCK, dtype=BF16)] * 2,
        scratch_shapes=square,
        compiler_params=PARAMS,
        name="left_root",
        cost_estimate=estimate(8 * 10**9),
    )(left, gradient)
    return pl.pallas_call(
        update_kernel,
        out_specs=pl.BlockSpec(memory_space=pl.ANY),
        out_shape=shape(height, width),
        scratch_shapes=whole,
        compiler_params=PARAMS,
        name="update",
    )(high, low, received)


def solution(mesh):
    names = ("yh", "yl", "x", "z", "core")
    fine = Mesh(mesh.devices.reshape(4, 2, 4, 8, 2), names)
    spec = P(names[:3], names[3:])
    return jax.shard_map(body, mesh=fine, in_specs=(spec,), out_specs=spec, check_vma=False)
```

```python
import functools

import jax
import jax.numpy as jnp
from jax import lax
from jax.experimental import pallas as pl
from jax.experimental.pallas import tpu as pltpu
from jax.sharding import Mesh, PartitionSpec as P

D_IN = 6144
D_OUT = 24576
BLOCK = 192
ITERS = 12
HALF = 96
LANES = 128
PACKED = 152
CHUNK = 2 * BLOCK
SCALE = (float(D_IN) * float(D_OUT)) ** 0.25
F32, BF16 = jnp.float32, jnp.bfloat16
PARAMS = pltpu.CompilerParams(vmem_limit_bytes=32 * 2**20)


def split(a):
    high = a.astype(BF16)
    return high, (a - high.astype(F32)).astype(BF16)


def dot(a, b, dims=((1,), (0,))):
    return lax.dot_general(a, b, (dims, ((), ())), preferred_element_type=F32)


def product(a, b, dims=((1,), (0,))):
    return dot(a[0], b[0], dims) + (dot(a[0], b[1], dims) + dot(a[1], b[0], dims))


def grid_of(height, width):
    shape = (height, width)
    return lax.broadcasted_iota(jnp.int32, shape, 0), lax.broadcasted_iota(jnp.int32, shape, 1)


def pack(a):
    tail = a[HALF:, HALF:]
    row, col = grid_of(HALF, LANES)
    wide = jnp.concatenate([tail, jnp.zeros((HALF, LANES - HALF), F32)], axis=1)
    top = jnp.where(col < row, wide, a[:HALF, :LANES])
    rest = a[:HALF, LANES:]
    diagonal = jnp.sum(jnp.where(row == col, wide, 0.0), axis=0, keepdims=True)
    return jnp.concatenate(
        [
            top,
            jnp.concatenate([rest[: HALF // 2], rest[HALF // 2 :]], axis=1),
            jnp.broadcast_to(diagonal, (8, LANES)),
        ],
        axis=0,
    )


def unpack(p):
    row, col = grid_of(HALF, HALF)
    upper = p[:HALF, :HALF]
    lower = upper.T
    middle = p[HALF : HALF + HALF // 2]
    rest = jnp.concatenate(
        [p[:HALF, HALF:], jnp.concatenate([middle[:, :64], middle[:, 64:]], axis=0)], axis=1
    )
    head = jnp.where(col < row, lower, upper)
    tail = jnp.where(col < row, upper, jnp.where(col == row, p[144:145, :HALF], lower))
    return jnp.concatenate(
        [jnp.concatenate([head, rest], axis=1), jnp.concatenate([rest.T, tail], axis=1)], axis=0
    )


def right_gram_kernel(grad_ref, right_ref):
    for c in range(right_ref.shape[0]):
        h = split(grad_ref[:, c * BLOCK : (c + 1) * BLOCK])
        right_ref[c] = pack(product(h, h, ((0,), (0,))))


def left_gram_kernel(grad_ref, left_ref):
    g = split(grad_ref[...])
    left_ref[...] = pack(product(g, g, ((1,), (1,))))


def newton(gram, m_ref, x_ref):
    row, col = grid_of(BLOCK, BLOCK)
    identity = (row == col).astype(F32)
    damped = gram + (0.01 / BLOCK * jnp.sum(gram * identity)) * identity
    norm = jnp.sqrt(jnp.sum(damped * damped, keepdims=True))
    m = damped / norm
    bands = [slice(0, HALF), slice(HALF, BLOCK)]

    def advance(m):
        parts = split(m)
        centred = (m - 0.5 * identity).astype(BF16)
        excess = [
            split(0.0625 * dot(centred[b], centred) - 0.015625 * identity[b] - 0.5625 * m[b])
            for b in bands
        ]
        halfway = [1.5625 * m[b] + product(e, parts) for e, b in zip(excess, bands)]
        whole = [jnp.concatenate([e[k] for e in excess], axis=0) for k in range(2)]
        return parts, jnp.concatenate([1.5625 * h + product(split(h), whole) for h in halfway], axis=0)

    def grow(parts):
        x = x_ref[...]
        return jnp.concatenate(
            [1.25 * x[b] - 0.25 * product(split(x[b]), parts) for b in bands], axis=0
        )

    x_ref[...] = (5.0 * identity - m) * 0.25
    m_ref[...] = advance(m)[1]

    def step(k, carry):
        parts, following = advance(m_ref[...])
        grown = grow(parts)
        m_ref[...] = following
        x_ref[...] = grown
        return carry

    lax.fori_loop(0, ITERS - 2, step, 0, unroll=True)
    return grow(split(m_ref[...])) * lax.rsqrt(jnp.sqrt(norm))


def right_root_kernel(parts_ref, roots_ref, m_ref, x_ref):
    total = functools.reduce(lambda a, b: a + b, [parts_ref[k] for k in range(parts_ref.shape[0])])
    root = pack(newton(unpack(total), m_ref, x_ref))
    for k in range(roots_ref.shape[0]):
        roots_ref[k] = root


def left_root_kernel(gram_ref, grad_ref, high_ref, low_ref, m_ref, x_ref):
    root = split(newton(unpack(gram_ref[...]), m_ref, x_ref))
    for k in range(grad_ref.shape[1] // CHUNK):
        mid = split(product(root, split(grad_ref[:, k * CHUNK : (k + 1) * CHUNK])))
        for c in range(CHUNK // BLOCK):
            window = slice(c * BLOCK, (c + 1) * BLOCK)
            high_ref[2 * k + c] = mid[0][:, window]
            low_ref[2 * k + c] = mid[1][:, window]


def halves(p):
    row, col = grid_of(HALF, HALF)
    found = []
    for part in split(p):
        square = part[:HALF, :HALF]
        none = jnp.zeros_like(square)
        middle = part[HALF : HALF + HALF // 2]
        rest = jnp.concatenate(
            [part[:HALF, HALF:], jnp.concatenate([middle[:, :64], middle[:, 64:]], axis=0)], axis=1
        )
        below = jnp.where(col < row, square, none)
        diagonal = jnp.broadcast_to(part[144:145, :HALF], (HALF, HALF))
        for head, tail in (
            (jnp.where(col >= row, square, none), jnp.where(col == row, diagonal, below)),
            (jnp.where(col > row, square, none), below),
        ):
            top = jnp.concatenate([head, rest], axis=1)
            found.append(jnp.concatenate([top, jnp.concatenate([none, tail], axis=1)], axis=0))
    return (found[0], found[2]), (found[1], found[3])


def update_kernel(high_ref, low_ref, roots_ref, out_ref, held, sems):
    stores = []
    for k in range(out_ref.shape[1] // CHUNK):
        for c in range(CHUNK // BLOCK):
            b = 2 * k + c
            mid = (high_ref[b], low_ref[b])
            plain, flipped = halves(roots_ref[b])
            block = product(mid, plain) + product(mid, flipped, ((1,), (1,)))
            held[k, :, c * BLOCK : (c + 1) * BLOCK] = block * SCALE
        stores.append(
            pltpu.make_async_copy(held.at[k], out_ref.at[:, pl.ds(k * CHUNK, CHUNK)], sems.at[k])
        )
        stores[-1].start()
    for store in stores:
        store.wait()


def shape(*dims, dtype=F32):
    return jax.ShapeDtypeStruct(dims, dtype)


def estimate(flops):
    return pl.CostEstimate(flops=flops, bytes_accessed=2**20, transcendentals=0)


def partner(x, axis, bits):
    return lax.ppermute(x, axis, [(i, i ^ bits) for i in range(lax.axis_size(axis))])


def swap(x, axes):
    return lax.all_to_all(x, axes, 0, 0, tiled=True)


def body(gradient):
    height, width = gradient.shape
    count = width // BLOCK
    chunks = width // CHUNK
    group = ("yl", "x")
    square = [pltpu.VMEM((BLOCK, BLOCK), F32)] * 2
    whole = [pltpu.VMEM((chunks, height, CHUNK), F32), pltpu.SemaphoreType.DMA((chunks,))]

    right = pl.pallas_call(
        right_gram_kernel,
        out_shape=shape(count, PACKED, LANES),
        compiler_params=PARAMS,
        name="right_gram",
    )(gradient)
    left = pl.pallas_call(
        left_gram_kernel,
        out_shape=shape(PACKED, LANES),
        compiler_params=PARAMS,
        name="left_gram",
        cost_estimate=estimate(10**9),
    )(gradient)
    right = swap(right, group)
    left = left + partner(left, "core", 1)
    left = left + partner(left, "z", 1)
    right, left = lax.optimization_barrier((jnp.sum(right, axis=0), left))
    rest = swap(jnp.broadcast_to(right[None], (lax.axis_size("yh"),) + right.shape), "yh")
    others = [partner(left, "z", bits) for bits in (2, 6, 4)]

    roots = pl.pallas_call(
        right_root_kernel,
        out_shape=shape(count, PACKED, LANES),
        scratch_shapes=square,
        compiler_params=PARAMS,
        name="right_root",
        cost_estimate=estimate(16 * 10**9),
    )(rest)
    roots, left, others = lax.optimization_barrier((roots, left, others))
    left = sum(others, left)
    received = swap(roots, group)

    high, low = pl.pallas_call(
        left_root_kernel,
        out_shape=[shape(count, height, BLOCK, dtype=BF16)] * 2,
        scratch_shapes=square,
        compiler_params=PARAMS,
        name="left_root",
        cost_estimate=estimate(8 * 10**9),
    )(left, gradient)
    return pl.pallas_call(
        update_kernel,
        out_specs=pl.BlockSpec(memory_space=pl.ANY),
        out_shape=shape(height, width),
        scratch_shapes=whole,
        compiler_params=PARAMS,
        name="update",
    )(high, low, received)


def solution(mesh):
    names = ("yh", "yl", "x", "z", "core")
    fine = Mesh(mesh.devices.reshape(4, 2, 4, 8, 2), names)
    spec = P(names[:3], names[3:])
    return jax.shard_map(body, mesh=fine, in_specs=(spec,), out_specs=spec, check_vma=False)
```
